32 devices in a mesh: row: 8 (over z, x), col: 4 (over y, core).
Axes of the slice: x: 2, y: 2, z: 4, core: 2. Of those that a mesh axis runs over, the one named last changes fastest.
Arguments:
- grad_out: bfloat16 [1536, 4096], P('row', 'col'), may hold values from -6 to 6
- w_down: bfloat16 [16384, 4096], P('row', 'col'), may hold values from -0.046875 to 0.046875
- pre_act: bfloat16 [1536, 16384], P('col', 'row'), may hold values from -6 to 6
- acc_down: float32 [16384, 4096], P('row', 'col'), may hold values from -4 to 4
Outputs:
- acc_new: float32 [16384, 4096], P('row', 'col')
- grad_pre: bfloat16 [1536, 16384], P('col', 'row')
The draws below stay inside these ranges and needn't reach their ends.
All inputs are finite; a program needn't handle non-finite values.
Results may differ from the reference program's by a relative error of at most 0.0023.
Values may be sent and summed in bfloat16 or wider, within the bound.
A program may use at most 128 MiB of HBM per device.

```python
import math
import jax
import jax.numpy as jnp
from jax import lax

D = 4096
FF = 16384
TOKENS = 1536


def level_of(stream_key, extent, pieces, smallest, top_value):
    factor_of, own = 1.0, jax.random.fold_in(stream_key, 6)
    for dim, parts in pieces:
        steps = jnp.exp(jax.random.uniform(jax.random.fold_in(own, dim), (parts,), jnp.float32, smallest / len(pieces), top_value / len(pieces)))
        factor_of = factor_of * jnp.repeat(steps, extent[dim] // parts).reshape([-1 if axis == dim else 1 for axis in range(len(extent))])
    return factor_of


def scatter_about(rng, shape, deviation, bound, split=(), kind=jnp.bfloat16):
    values = deviation * jax.random.normal(rng, shape, jnp.float32)
    if split:
        values = values * level_of(rng, shape, split, -0.22, 0.18)
    return jnp.clip(values, -bound, bound).astype(kind)


def setup_inputs(seed: int = 0) -> dict:
    splits = jax.random.split(jax.random.key(seed), 5)
    grad_out = scatter_about(splits[0], (TOKENS, D), 1.0, 6.0, ((0, 8), (1, 4)))
    w_down = scatter_about(splits[1], (FF, D), FF ** -0.5, 0.046875, ((0, 8), (1, 4)))
    pre_act = scatter_about(splits[2], (TOKENS, FF), 1.0, 6.0, ((0, 4), (1, 8)))
    acc_down = scatter_about(splits[3], (FF, D), 0.5, 4.0, ((0, 8), (1, 4)), jnp.float32)
    return dict(grad_out=grad_out, w_down=w_down, pre_act=pre_act, acc_down=acc_down)


def gelu_value(v):
    return 0.5 * v * (1.0 + lax.erf(v / math.sqrt(2.0)))

def gelu_slope(v):
    return 0.5 * (1.0 + lax.erf(v / math.sqrt(2.0))) + v * jnp.exp(-0.5 * v * v) / math.sqrt(2.0 * math.pi)

def reference(grad_out, w_down, pre_act, acc_down):
    pre_float = pre_act.astype(jnp.float32)
    act = gelu_value(pre_float).astype(jnp.bfloat16)
    grad_act = lax.dot_general(grad_out, w_down, (((1,), (1,)), ((), ())), preferred_element_type=jnp.float32)
    grad_pre = (grad_act * gelu_slope(pre_float)).astype(jnp.bfloat16)
    grad_w = lax.dot_general(act, grad_out, (((0,), (0,)), ((), ())), preferred_element_type=jnp.float32)
    acc_new = acc_down + grad_w * float(TOKENS) ** (-0.5)
    return (acc_new, grad_pre)
```

```python
import math

import jax
import jax.numpy as jnp
from jax import lax
from jax.sharding import PartitionSpec as P

F16_TOP = 30000.0
CHUNKS = 4


def gelu_value(v):
    return 0.5 * v * (1.0 + lax.erf(v / math.sqrt(2.0)))


def gelu_slope(v):
    return 0.5 * (1.0 + lax.erf(v / math.sqrt(2.0))) + v * jnp.exp(-0.5 * v * v) / math.sqrt(
        2.0 * math.pi
    )


def on_device_plain(grad_out, w_down, pre_act, acc_down):
    total = grad_out.shape[0] * lax.axis_size("row")
    pre_float = pre_act.astype(jnp.float32)
    pre_full = lax.all_gather(pre_act, "col", axis=0, tiled=True)
    act_full = gelu_value(pre_full.astype(jnp.float32)).astype(jnp.bfloat16)
    piece = lax.all_gather(grad_out, "row", axis=0, tiled=True)
    block = lax.dot_general(
        piece, w_down, (((1,), (1,)), ((), ())), preferred_element_type=jnp.float32
    )
    grad_w = lax.dot_general(
        act_full, piece, (((0,), (0,)), ((), ())), preferred_element_type=jnp.float32
    )
    summed = lax.psum_scatter(block, "col", scatter_dimension=0, tiled=True)
    grad_pre = (summed * gelu_slope(pre_float)).astype(jnp.bfloat16)
    acc_new = acc_down + grad_w * float(total) ** (-0.5)
    return (acc_new, grad_pre)


def matmul_t(a, b):
    return lax.dot_general(a, b, (((1,), (1,)), ((), ())), preferred_element_type=jnp.float32)


def on_device_paired(grad_out, w_down, pre_act, acc_down):
    rows, feats = grad_out.shape
    hidden = w_down.shape[0]
    tokens = pre_act.shape[0]
    total = rows * 8
    row, col = lax.axis_index("row"), lax.axis_index("col")
    z, x = row // 2, row % 2
    y, core = col // 2, col % 2
    over_y = [(i, i ^ 2) for i in range(4)]
    over_core = [(i, i ^ 1) for i in range(4)]
    over_x = [(i, i ^ 1) for i in range(8)]
    next_z = [(i, (i + 2) % 8) for i in range(8)]

    pre_far = lax.ppermute(pre_act, "col", over_y)

    tops = jnp.stack([
        jnp.max(jnp.abs(grad_out.astype(jnp.float32))),
        jnp.max(jnp.abs(w_down.astype(jnp.float32))),
    ])
    tops = lax.pmax(tops, ("row", "col"))
    scale = F16_TOP / jnp.maximum(2.0 * feats * tops[0] * tops[1], 1e-30)
    unscale = 1.0 / scale

    shard = grad_out
    piece = jnp.zeros((4, 2, rows, feats), jnp.bfloat16)
    for k in range(4):
        zk = (z + 4 - k) % 4
        other = lax.ppermute(shard, "row", over_x)
        piece = lax.dynamic_update_slice(piece, shard[None, None], (zk, x, 0, 0))
        piece = lax.dynamic_update_slice(piece, other[None, None], (zk, 1 - x, 0, 0))
        if k < 3:
            shard = lax.ppermute(shard, "row", next_z)
    piece = piece.reshape(4, 2 * rows, feats)

    def block_of(b):
        return lax.dynamic_index_in_dim(piece, b, 0, keepdims=False)

    far_mine, far_sib = block_of(2 * (1 - y) + core), block_of(2 * (1 - y) + 1 - core)
    near_mine, near_sib = block_of(2 * y + core), block_of(2 * y + 1 - core)
    width = hidden // CHUNKS
    arrived = []
    for j in range(CHUNKS):
        w = w_down[j * width:(j + 1) * width]
        out = (matmul_t(far_sib, w) * scale).astype(jnp.float16)
        back = lax.ppermute(out, "col", over_core)
        pair = matmul_t(far_mine, w) * scale + back.astype(jnp.float32)
        arrived.append(lax.ppermute(pair.astype(jnp.float16), "col", over_y))

    act = gelu_value(jnp.stack([pre_act, pre_far]).astype(jnp.float32)).astype(jnp.bfloat16)
    act_sib = lax.ppermute(act, "col", over_core)

    near_out = (matmul_t(near_sib, w_down) * scale).astype(jnp.float16)
    near_back = lax.ppermute(near_out, "col", over_core)
    near = matmul_t(near_mine, w_down) * scale + near_back.astype(jnp.float32)

    act_full = jnp.concatenate([act[0], act[1], act_sib[0], act_sib[1]], axis=0)
    piece_full = jnp.concatenate([near_mine, far_mine, near_sib, far_sib], axis=0)
    grad_w = lax.dot_general(
        act_full, piece_full, (((0,), (0,)), ((), ())), preferred_element_type=jnp.float32
    )
    acc_new = acc_down + grad_w * float(total) ** (-0.5)

    slope = gelu_slope(pre_act.astype(jnp.float32))
    parts = []
    for j in range(CHUNKS):
        cut = slice(j * width, (j + 1) * width)
        both = (near[:, cut] + arrived[j].astype(jnp.float32)) * unscale
        parts.append((both * slope[:, cut]).astype(jnp.bfloat16))
    return (acc_new, jnp.concatenate(parts, axis=1))


def solution(mesh):
    paired = mesh.shape["row"] == 8 and mesh.shape["col"] == 4
    return jax.shard_map(
        on_device_paired if paired else on_device_plain,
        mesh=mesh,
        in_specs=(P("row", "col"), P("row", "col"), P("col", "row"), P("row", "col")),
        out_specs=(P("row", "col"), P("col", "row")),
        check_vma=False,
    )
```

```python
import math

import jax
import jax.numpy as jnp
from jax import lax
from jax.sharding import PartitionSpec as P

F16_TOP = 30000.0
CHUNKS = 4


def gelu_value(v):
    return 0.5 * v * (1.0 + lax.erf(v / math.sqrt(2.0)))


def gelu_slope(v):
    return 0.5 * (1.0 + lax.erf(v / math.sqrt(2.0))) + v * jnp.exp(-0.5 * v * v) / math.sqrt(
        2.0 * math.pi
    )


def on_device_plain(grad_out, w_down, pre_act, acc_down):
    total = grad_out.shape[0] * lax.axis_size("row")
    pre_float = pre_act.astype(jnp.float32)
    pre_full = lax.all_gather(pre_act, "col", axis=0, tiled=True)
    act_full = gelu_value(pre_full.astype(jnp.float32)).astype(jnp.bfloat16)
    piece = lax.all_gather(grad_out, "row", axis=0, tiled=True)
    block = lax.dot_general(
        piece, w_down, (((1,), (1,)), ((), ())), preferred_element_type=jnp.float32
    )
    grad_w = lax.dot_general(
        act_full, piece, (((0,), (0,)), ((), ())), preferred_element_type=jnp.float32
    )
    summed = lax.psum_scatter(block, "col", scatter_dimension=0, tiled=True)
    grad_pre = (summed * gelu_slope(pre_float)).astype(jnp.bfloat16)
    acc_new = acc_down + grad_w * float(total) ** (-0.5)
    return (acc_new, grad_pre)


def matmul_t(a, b):
    return lax.dot_general(a, b, (((1,), (1,)), ((), ())), preferred_element_type=jnp.float32)


def on_device_paired(grad_out, w_down, pre_act, acc_down):
    rows, feats = grad_out.shape
    hidden = w_down.shape[0]
    tokens = pre_act.shape[0]
    total = rows * 8
    row, col = lax.axis_index("row"), lax.axis_index("col")
    z, x = row // 2, row % 2
    y, core = col // 2, col % 2
    over_y = [(i, i ^ 2) for i in range(4)]
    over_core = [(i, i ^ 1) for i in range(4)]
    over_x = [(i, i ^ 1) for i in range(8)]
    next_z = [(i, (i + 2) % 8) for i in range(8)]

    pre_far = lax.ppermute(pre_act, "col", over_y)

    def top(v):
        return jnp.max(jnp.abs(v)).astype(jnp.float32)

    w_top = top(w_down)
    g_top = top(grad_out)

    shard = grad_out
    piece = jnp.zeros((4, 2, rows, feats), jnp.bfloat16)
    for k in range(4):
        zk = (z + 4 - k) % 4
        other = lax.ppermute(shard, "row", over_x)
        piece = lax.dynamic_update_slice(piece, shard[None, None], (zk, x, 0, 0))
        piece = lax.dynamic_update_slice(piece, other[None, None], (zk, 1 - x, 0, 0))
        g_top = jnp.maximum(g_top, jnp.maximum(top(shard), top(other)))
        if k < 3:
            shard = lax.ppermute(shard, "row", next_z)
    piece = piece.reshape(4, 2 * rows, feats)

    bound = jnp.full((8, 128), jnp.maximum(feats * g_top * w_top, 1e-30))
    bound_sib = lax.ppermute(bound, "col", over_core)
    bound_pair = bound + bound_sib
    bound_far = lax.ppermute(bound_pair, "col", over_y)
    scale, from_sib = F16_TOP / bound[0, 0], bound_sib[0, 0] / F16_TOP
    to_far, from_far = F16_TOP / bound_pair[0, 0], bound_far[0, 0] / F16_TOP

    def block_of(b):
        return lax.dynamic_index_in_dim(piece, b, 0, keepdims=False)

    far_mine, far_sib = block_of(2 * (1 - y) + core), block_of(2 * (1 - y) + 1 - core)
    near_mine, near_sib = block_of(2 * y + core), block_of(2 * y + 1 - core)
    width = hidden // CHUNKS
    pairs = []
    for j in range(CHUNKS):
        w = w_down[j * width:(j + 1) * width]
        out = (matmul_t(far_sib, w) * scale).astype(jnp.float16)
        back = lax.ppermute(out, "col", over_core)
        pair = matmul_t(far_mine, w) + back.astype(jnp.float32) * from_sib
        pairs.append((pair * to_far).astype(jnp.float16))
    arrived = [lax.ppermute(pair, "col", over_y) for pair in pairs[:-1]]

    act = gelu_value(jnp.stack([pre_act, pre_far]).astype(jnp.float32)).astype(jnp.bfloat16)
    act_sib = lax.ppermute(act, "col", over_core)

    near_out = (matmul_t(near_sib, w_down) * scale).astype(jnp.float16)
    near_back = lax.ppermute(near_out, "col", over_core)
    near = matmul_t(near_mine, w_down) + near_back.astype(jnp.float32) * from_sib

    act_full = jnp.concatenate([act[0], act[1], act_sib[0], act_sib[1]], axis=0)
    piece_full = jnp.concatenate([near_mine, far_mine, near_sib, far_sib], axis=0)
    grad_w = lax.dot_general(
        act_full, piece_full, (((0,), (0,)), ((), ())), preferred_element_type=jnp.float32
    )
    acc_new = acc_down + grad_w * float(total) ** (-0.5)

    last, acc_new = lax.optimization_barrier((pairs[-1], acc_new))
    arrived.append(lax.ppermute(last, "col", over_y))

    slope = gelu_slope(pre_act.astype(jnp.float32))
    parts = []
    for j in range(CHUNKS):
        cut = slice(j * width, (j + 1) * width)
        both = near[:, cut] + arrived[j].astype(jnp.float32) * from_far
        parts.append((both * slope[:, cut]).astype(jnp.bfloat16))
    return (acc_new, jnp.concatenate(parts, axis=1))


def solution(mesh):
    paired = mesh.shape["row"] == 8 and mesh.shape["col"] == 4
    return jax.shard_map(
        on_device_paired if paired else on_device_plain,
        mesh=mesh,
        in_specs=(P("row", "col"), P("row", "col"), P("col", "row"), P("row", "col")),
        out_specs=(P("row", "col"), P("col", "row")),
        check_vma=False,
    )
```

```python
import math

import jax
import jax.numpy as jnp
from jax import lax
from jax.sharding import PartitionSpec as P

F16_TOP = 30000.0
CHUNKS = 4


def gelu_value(v):
    return 0.5 * v * (1.0 + lax.erf(v / math.sqrt(2.0)))


def gelu_slope(v):
    return 0.5 * (1.0 + lax.erf(v / math.sqrt(2.0))) + v * jnp.exp(-0.5 * v * v) / math.sqrt(
        2.0 * math.pi
    )


def on_device_plain(grad_out, w_down, pre_act, acc_down):
    total = grad_out.shape[0] * lax.axis_size("row")
    pre_float = pre_act.astype(jnp.float32)
    pre_full = lax.all_gather(pre_act, "col", axis=0, tiled=True)
    act_full = gelu_value(pre_full.astype(jnp.float32)).astype(jnp.bfloat16)
    piece = lax.all_gather(grad_out, "row", axis=0, tiled=True)
    block = lax.dot_general(
        piece, w_down, (((1,), (1,)), ((), ())), preferred_element_type=jnp.float32
    )
    grad_w = lax.dot_general(
        act_full, piece, (((0,), (0,)), ((), ())), preferred_element_type=jnp.float32
    )
    summed = lax.psum_scatter(block, "col", scatter_dimension=0, tiled=True)
    grad_pre = (summed * gelu_slope(pre_float)).astype(jnp.bfloat16)
    acc_new = acc_down + grad_w * float(total) ** (-0.5)
    return (acc_new, grad_pre)


def matmul_t(a, b):
    return lax.dot_general(a, b, (((1,), (1,)), ((), ())), preferred_element_type=jnp.float32)


def on_device_paired(grad_out, w_down, pre_act, acc_down):
    rows, feats = grad_out.shape
    hidden = w_down.shape[0]
    tokens = pre_act.shape[0]
    total = rows * 8
    row, col = lax.axis_index("row"), lax.axis_index("col")
    z, x = row // 2, row % 2
    y, core = col // 2, col % 2
    over_y = [(i, i ^ 2) for i in range(4)]
    over_core = [(i, i ^ 1) for i in range(4)]
    over_x = [(i, i ^ 1) for i in range(8)]
    next_z = [(i, (i + 2) % 8) for i in range(8)]

    pre_far = lax.ppermute(pre_act, "col", over_y)

    def top(v):
        return jnp.max(jnp.abs(v)).astype(jnp.float32)

    w_top = top(w_down)
    g_top = top(grad_out)

    act_near = gelu_value(pre_act.astype(jnp.float32)).astype(jnp.bfloat16)
    act_near_sib = lax.ppermute(act_near, "col", over_core)

    shard = grad_out
    piece = jnp.zeros((4, 2, rows, feats), jnp.bfloat16)
    for k in range(4):
        zk = (z + 4 - k) % 4
        place = jnp.where(zk // 2 == y, 2, 0) + jnp.where(zk % 2 == core, 1, 0)
        other = lax.ppermute(shard, "row", over_x)
        piece = lax.dynamic_update_slice(piece, shard[None, None], (place, x, 0, 0))
        piece = lax.dynamic_update_slice(piece, other[None, None], (place, 1 - x, 0, 0))
        g_top = jnp.maximum(g_top, jnp.maximum(top(shard), top(other)))
        if k < 3:
            shard = lax.ppermute(shard, "row", next_z)
    piece = piece.reshape(4 * tokens, feats)

    bound = jnp.full((8, 128), jnp.maximum(feats * g_top * w_top, 1e-30))
    bound_sib = lax.ppermute(bound, "col", over_core)
    bound_pair = bound + bound_sib
    bound_far = lax.ppermute(bound_pair, "col", over_y)
    scale, from_sib = F16_TOP / bound[0, 0], bound_sib[0, 0] / F16_TOP
    to_far, from_far = F16_TOP / bound_pair[0, 0], bound_far[0, 0] / F16_TOP

    far_sib, far_mine = piece[:tokens], piece[tokens:2 * tokens]
    near_sib, near_mine = piece[2 * tokens:3 * tokens], piece[3 * tokens:]
    width = hidden // CHUNKS
    pairs = []
    for j in range(CHUNKS):
        w = w_down[j * width:(j + 1) * width]
        out = (matmul_t(far_sib, w) * scale).astype(jnp.float16)
        back = lax.ppermute(out, "col", over_core)
        pair = matmul_t(far_mine, w) + back.astype(jnp.float32) * from_sib
        pairs.append((pair * to_far).astype(jnp.float16))
    arrived = [lax.ppermute(pair, "col", over_y) for pair in pairs[:-1]]

    act_far = gelu_value(pre_far.astype(jnp.float32)).astype(jnp.bfloat16)
    act_far, near_sib, _ = lax.optimization_barrier((act_far, near_sib, pairs[1]))
    act_far_sib = lax.ppermute(act_far, "col", over_core)

    near_out = (matmul_t(near_sib, w_down) * scale).astype(jnp.float16)
    near_back = lax.ppermute(near_out, "col", over_core)
    near = matmul_t(near_mine, w_down) + near_back.astype(jnp.float32) * from_sib

    act_full = jnp.concatenate([act_far_sib, act_far, act_near_sib, act_near], axis=0)
    grad_w = lax.dot_general(
        act_full, piece, (((0,), (0,)), ((), ())), preferred_element_type=jnp.float32
    )
    acc_new = acc_down + grad_w * float(total) ** (-0.5)

    last, acc_new = lax.optimization_barrier((pairs[-1], acc_new))
    arrived.append(lax.ppermute(last, "col", over_y))

    slope = gelu_slope(pre_act.astype(jnp.float32))
    parts = []
    for j in range(CHUNKS):
        cut = slice(j * width, (j + 1) * width)
        mine, factor, there = near[:, cut], slope[:, cut], arrived[j]
        if j == CHUNKS - 1:
            mine, factor, there, *parts = lax.optimization_barrier((mine, factor, there, *parts))
        both = mine + there.astype(jnp.float32) * from_far
        parts.append((both * factor).astype(jnp.bfloat16))
    return (acc_new, jnp.concatenate(parts, axis=1))


def solution(mesh):
    paired = mesh.shape["row"] == 8 and mesh.shape["col"] == 4
    return jax.shard_map(
        on_device_paired if paired else on_device_plain,
        mesh=mesh,
        in_specs=(P("row", "col"), P("row", "col"), P("col", "row"), P("row", "col")),
        out_specs=(P("row", "col"), P("col", "row")),
        check_vma=False,
    )
```

```python
import math

import jax
import jax.numpy as jnp
from jax import lax
from jax.sharding import PartitionSpec as P

F16_TOP = 30000.0
CHUNKS = 4


def gelu_value(v):
    return 0.5 * v * (1.0 + lax.erf(v / math.sqrt(2.0)))


def gelu_slope(v):
    return 0.5 * (1.0 + lax.erf(v / math.sqrt(2.0))) + v * jnp.exp(-0.5 * v * v) / math.sqrt(
        2.0 * math.pi
    )


def on_device_plain(grad_out, w_down, pre_act, acc_down):
    total = grad_out.shape[0] * lax.axis_size("row")
    pre_float = pre_act.astype(jnp.float32)
    pre_full = lax.all_gather(pre_act, "col", axis=0, tiled=True)
    act_full = gelu_value(pre_full.astype(jnp.float32)).astype(jnp.bfloat16)
    piece = lax.all_gather(grad_out, "row", axis=0, tiled=True)
    block = lax.dot_general(
        piece, w_down, (((1,), (1,)), ((), ())), preferred_element_type=jnp.float32
    )
    grad_w = lax.dot_general(
        act_full, piece, (((0,), (0,)), ((), ())), preferred_element_type=jnp.float32
    )
    summed = lax.psum_scatter(block, "col", scatter_dimension=0, tiled=True)
    grad_pre = (summed * gelu_slope(pre_float)).astype(jnp.bfloat16)
    acc_new = acc_down + grad_w * float(total) ** (-0.5)
    return (acc_new, grad_pre)


def matmul_t(a, b):
    return lax.dot_general(a, b, (((1,), (1,)), ((), ())), preferred_element_type=jnp.float32)


def on_device_paired(grad_out, w_down, pre_act, acc_down):
    rows, feats = grad_out.shape
    hidden = w_down.shape[0]
    tokens = pre_act.shape[0]
    total = rows * 8
    row, col = lax.axis_index("row"), lax.axis_index("col")
    z, x = row // 2, row % 2
    y, core = col // 2, col % 2
    over_y = [(i, i ^ 2) for i in range(4)]
    over_core = [(i, i ^ 1) for i in range(4)]
    over_x = [(i, i ^ 1) for i in range(8)]
    next_z = [(i, (i + 2) % 8) for i in range(8)]

    pre_far = lax.ppermute(pre_act, "col", over_y)

    def top(v):
        return jnp.max(jnp.abs(v)).astype(jnp.float32)

    upper = lax.broadcasted_iota(jnp.int32, (8, 128), 0) < 4
    tops = jnp.where(upper, top(grad_out), top(w_down))
    for axis, perm in (
        ("col", over_core),
        ("row", next_z),
        ("row", [(i, (i + 4) % 8) for i in range(8)]),
        ("row", over_x),
        ("col", over_y),
    ):
        tops = jnp.maximum(tops, lax.ppermute(tops, axis, perm))
    bound = jnp.maximum(2.0 * feats * tops[0, 0] * tops[7, 0], 1e-30)
    scale, unscale = F16_TOP / bound, bound / F16_TOP

    act_near = gelu_value(pre_act.astype(jnp.float32)).astype(jnp.bfloat16)
    act_near_sib = lax.ppermute(act_near, "col", over_core)

    shard, other = grad_out, None
    half = rows // 2
    piece = jnp.zeros((4, 2, rows, feats), jnp.bfloat16)
    for k in range(4):
        zk = (z + 4 - k) % 4
        place = jnp.where(zk // 2 == y, 2, 0) + jnp.where(zk % 2 == core, 1, 0)
        if k < 3:
            after = lax.ppermute(shard, "row", next_z)
            other = lax.ppermute(shard, "row", over_x)
            piece = lax.dynamic_update_slice(piece, shard[None, None], (place, x, 0, 0))
            piece = lax.dynamic_update_slice(piece, other[None, None], (place, 1 - x, 0, 0))
            shard = after
        else:
            first = lax.ppermute(shard[:half], "row", over_x)
            second = lax.ppermute(other[half:], "row", next_z)
            piece = lax.dynamic_update_slice(piece, shard[None, None], (place, x, 0, 0))
            piece = lax.dynamic_update_slice(piece, first[None, None], (place, 1 - x, 0, 0))
            piece = lax.dynamic_update_slice(piece, second[None, None], (place, 1 - x, half, 0))
    piece = piece.reshape(4 * tokens, feats)

    far_sib, far_mine = piece[:tokens], piece[tokens:2 * tokens]
    near_sib, near_mine = piece[2 * tokens:3 * tokens], piece[3 * tokens:]
    width = hidden // CHUNKS
    pairs = []
    for j in range(CHUNKS):
        w = w_down[j * width:(j + 1) * width]
        out = (matmul_t(far_sib, w) * scale).astype(jnp.float16)
        back = lax.ppermute(out, "col", over_core)
        pair = matmul_t(far_mine, w) * scale + back.astype(jnp.float32)
        pairs.append(pair.astype(jnp.float16))
    arrived = [lax.ppermute(pair, "col", over_y) for pair in pairs[:-1]]

    act_far = gelu_value(pre_far.astype(jnp.float32)).astype(jnp.bfloat16)
    act_far, near_sib, _ = lax.optimization_barrier((act_far, near_sib, pairs[1]))
    act_far_sib = lax.ppermute(act_far, "col", over_core)

    near_out = (matmul_t(near_sib, w_down) * scale).astype(jnp.float16)
    near_back = lax.ppermute(near_out, "col", over_core)
    near = matmul_t(near_mine, w_down) + near_back.astype(jnp.float32) * unscale

    act_full = jnp.concatenate([act_far_sib, act_far, act_near_sib, act_near], axis=0)
    grad_w = lax.dot_general(
        act_full, piece, (((0,), (0,)), ((), ())), preferred_element_type=jnp.float32
    )
    acc_new = acc_down + grad_w * float(total) ** (-0.5)

    last, acc_new = lax.optimization_barrier((pairs[-1], acc_new))
    arrived.append(lax.ppermute(last, "col", over_y))

    slope = gelu_slope(pre_act.astype(jnp.float32))
    parts = []
    for j in range(CHUNKS):
        cut = slice(j * width, (j + 1) * width)
        mine, factor, there = near[:, cut], slope[:, cut], arrived[j]
        if j == CHUNKS - 1:
            mine, factor, there, *parts = lax.optimization_barrier((mine, factor, there, *parts))
        both = mine + there.astype(jnp.float32) * unscale
        parts.append((both * factor).astype(jnp.bfloat16))
    return (acc_new, jnp.concatenate(parts, axis=1))


def solution(mesh):
    paired = mesh.shape["row"] == 8 and mesh.shape["col"] == 4
    return jax.shard_map(
        on_device_paired if paired else on_device_plain,
        mesh=mesh,
        in_specs=(P("row", "col"), P("row", "col"), P("col", "row"), P("row", "col")),
        out_specs=(P("row", "col"), P("col", "row")),
        check_vma=False,
    )
```

```python
import math

import jax
import jax.numpy as jnp
from jax import lax
from jax.sharding import PartitionSpec as P

F16_TOP = 30000.0
CHUNKS = 4


def gelu_value(v):
    return 0.5 * v * (1.0 + lax.erf(v / math.sqrt(2.0)))


def gelu_slope(v):
    return 0.5 * (1.0 + lax.erf(v / math.sqrt(2.0))) + v * jnp.exp(-0.5 * v * v) / math.sqrt(
        2.0 * math.pi
    )


def on_device_plain(grad_out, w_down, pre_act, acc_down):
    total = grad_out.shape[0] * lax.axis_size("row")
    pre_float = pre_act.astype(jnp.float32)
    pre_full = lax.all_gather(pre_act, "col", axis=0, tiled=True)
    act_full = gelu_value(pre_full.astype(jnp.float32)).astype(jnp.bfloat16)
    piece = lax.all_gather(grad_out, "row", axis=0, tiled=True)
    block = lax.dot_general(
        piece, w_down, (((1,), (1,)), ((), ())), preferred_element_type=jnp.float32
    )
    grad_w = lax.dot_general(
        act_full, piece, (((0,), (0,)), ((), ())), preferred_element_type=jnp.float32
    )
    summed = lax.psum_scatter(block, "col", scatter_dimension=0, tiled=True)
    grad_pre = (summed * gelu_slope(pre_float)).astype(jnp.bfloat16)
    acc_new = acc_down + grad_w * float(total) ** (-0.5)
    return (acc_new, grad_pre)


def matmul_t(a, b):
    return lax.dot_general(a, b, (((1,), (1,)), ((), ())), preferred_element_type=jnp.float32)


def on_device_paired(grad_out, w_down, pre_act, acc_down):
    rows, feats = grad_out.shape
    hidden = w_down.shape[0]
    tokens = pre_act.shape[0]
    total = rows * 8
    row, col = lax.axis_index("row"), lax.axis_index("col")
    z, x = row // 2, row % 2
    y, core = col // 2, col % 2
    over_y = [(i, i ^ 2) for i in range(4)]
    over_core = [(i, i ^ 1) for i in range(4)]
    over_x = [(i, i ^ 1) for i in range(8)]
    next_z = [(i, (i + 2) % 8) for i in range(8)]

    pre_far = lax.ppermute(pre_act, "col", over_y)

    def top(v):
        return jnp.max(jnp.abs(v)).astype(jnp.float32)

    w_top = top(w_down)
    g_top = top(grad_out)

    act_near = gelu_value(pre_act.astype(jnp.float32)).astype(jnp.bfloat16)
    act_near_sib = lax.ppermute(act_near, "col", over_core)

    shard, other = grad_out, None
    half = rows // 2
    piece = jnp.zeros((4, 2, rows, feats), jnp.bfloat16)
    for k in range(4):
        zk = (z + 4 - k) % 4
        place = jnp.where(zk // 2 == y, 2, 0) + jnp.where(zk % 2 == core, 1, 0)
        if k < 3:
            after = lax.ppermute(shard, "row", next_z)
            other = lax.ppermute(shard, "row", over_x)
            piece = lax.dynamic_update_slice(piece, shard[None, None], (place, x, 0, 0))
            piece = lax.dynamic_update_slice(piece, other[None, None], (place, 1 - x, 0, 0))
            g_top = jnp.maximum(g_top, jnp.maximum(top(after), top(other)))
            shard = after
        else:
            first = lax.ppermute(shard[:half], "row", over_x)
            second = lax.ppermute(other[half:], "row", next_z)
            piece = lax.dynamic_update_slice(piece, shard[None, None], (place, x, 0, 0))
            piece = lax.dynamic_update_slice(piece, first[None, None], (place, 1 - x, 0, 0))
            piece = lax.dynamic_update_slice(piece, second[None, None], (place, 1 - x, half, 0))
            g_top = jnp.maximum(g_top, jnp.maximum(top(first), top(second)))
    piece = piece.reshape(4 * tokens, feats)

    bound = jnp.full((8, 128), jnp.maximum(feats * g_top * w_top, 1e-30))
    bound_sib = lax.ppermute(bound, "col", over_core)
    bound_pair = bound + bound_sib
    bound_far = lax.ppermute(bound_pair, "col", over_y)
    scale, from_sib = F16_TOP / bound[0, 0], bound_sib[0, 0] / F16_TOP
    to_far, from_far = F16_TOP / bound_pair[0, 0], bound_far[0, 0] / F16_TOP

    far_sib, far_mine = piece[:tokens], piece[tokens:2 * tokens]
    near_sib, near_mine = piece[2 * tokens:3 * tokens], piece[3 * tokens:]
    width = hidden // CHUNKS
    pairs = []
    for j in range(CHUNKS):
        w = w_down[j * width:(j + 1) * width]
        out = (matmul_t(far_sib, w) * scale).astype(jnp.float16)
        back = lax.ppermute(out, "col", over_core)
        pair = matmul_t(far_mine, w) + back.astype(jnp.float32) * from_sib
        pairs.append((pair * to_far).astype(jnp.float16))
    arrived = [lax.ppermute(pair, "col", over_y) for pair in pairs[:-1]]

    act_far = gelu_value(pre_far.astype(jnp.float32)).astype(jnp.bfloat16)
    act_far, near_sib, _ = lax.optimization_barrier((act_far, near_sib, pairs[2]))
    act_far_sib = lax.ppermute(act_far, "col", over_core)

    near_out = (matmul_t(near_sib, w_down) * scale).astype(jnp.float16)
    near_back = lax.ppermute(near_out, "col", over_core)
    near = matmul_t(near_mine, w_down) + near_back.astype(jnp.float32) * from_sib

    act_full = jnp.concatenate([act_far_sib, act_far, act_near_sib, act_near], axis=0)
    grad_w = lax.dot_general(
        act_full, piece, (((0,), (0,)), ((), ())), preferred_element_type=jnp.float32
    )
    acc_new = acc_down + grad_w * float(total) ** (-0.5)

    last, acc_new = lax.optimization_barrier((pairs[-1], acc_new))
    arrived.append(lax.ppermute(last, "col", over_y))

    slope = gelu_slope(pre_act.astype(jnp.float32))
    parts = []
    for j in range(CHUNKS):
        cut = slice(j * width, (j + 1) * width)
        mine, factor, there = near[:, cut], slope[:, cut], arrived[j]
        if j == CHUNKS - 1:
            mine, factor, there, *parts = lax.optimization_barrier((mine, factor, there, *parts))
        both = mine + there.astype(jnp.float32) * from_far
        parts.append((both * factor).astype(jnp.bfloat16))
    return (acc_new, jnp.concatenate(parts, axis=1))


def solution(mesh):
    paired = mesh.shape["row"] == 8 and mesh.shape["col"] == 4
    return jax.shard_map(
        on_device_paired if paired else on_device_plain,
        mesh=mesh,
        in_specs=(P("row", "col"), P("row", "col"), P("col", "row"), P("row", "col")),
        out_specs=(P("row", "col"), P("col", "row")),
        check_vma=False,
    )
```

```python
import math

import jax
import jax.numpy as jnp
from jax import lax
from jax.sharding import PartitionSpec as P

F16_TOP = 30000.0
CHUNKS = 4


def gelu_value(v):
    return 0.5 * v * (1.0 + lax.erf(v / math.sqrt(2.0)))


def gelu_slope(v):
    return 0.5 * (1.0 + lax.erf(v / math.sqrt(2.0))) + v * jnp.exp(-0.5 * v * v) / math.sqrt(
        2.0 * math.pi
    )


def on_device_plain(grad_out, w_down, pre_act, acc_down):
    total = grad_out.shape[0] * lax.axis_size("row")
    pre_float = pre_act.astype(jnp.float32)
    pre_full = lax.all_gather(pre_act, "col", axis=0, tiled=True)
    act_full = gelu_value(pre_full.astype(jnp.float32)).astype(jnp.bfloat16)
    piece = lax.all_gather(grad_out, "row", axis=0, tiled=True)
    block = lax.dot_general(
        piece, w_down, (((1,), (1,)), ((), ())), preferred_element_type=jnp.float32
    )
    grad_w = lax.dot_general(
        act_full, piece, (((0,), (0,)), ((), ())), preferred_element_type=jnp.float32
    )
    summed = lax.psum_scatter(block, "col", scatter_dimension=0, tiled=True)
    grad_pre = (summed * gelu_slope(pre_float)).astype(jnp.bfloat16)
    acc_new = acc_down + grad_w * float(total) ** (-0.5)
    return (acc_new, grad_pre)


def matmul_t(a, b):
    return lax.dot_general(a, b, (((1,), (1,)), ((), ())), preferred_element_type=jnp.float32)


def on_device_paired(grad_out, w_down, pre_act, acc_down):
    rows, feats = grad_out.shape
    hidden = w_down.shape[0]
    tokens = pre_act.shape[0]
    total = rows * 8
    row, col = lax.axis_index("row"), lax.axis_index("col")
    z, x = row // 2, row % 2
    y, core = col // 2, col % 2
    over_y = [(i, i ^ 2) for i in range(4)]
    over_core = [(i, i ^ 1) for i in range(4)]
    over_x = [(i, i ^ 1) for i in range(8)]
    next_z = [(i, (i + 2) % 8) for i in range(8)]

    pre_far = lax.ppermute(pre_act, "col", over_y)

    def top(v):
        return jnp.max(jnp.abs(v)).astype(jnp.float32)

    w_top = top(w_down)
    g_top = top(grad_out)

    act_near = gelu_value(pre_act.astype(jnp.float32)).astype(jnp.bfloat16)
    act_near_sib = lax.ppermute(act_near, "col", over_core)

    shard = grad_out
    piece = jnp.zeros((4, 2, rows, feats), jnp.bfloat16)
    for k in range(4):
        zk = (z + 4 - k) % 4
        place = jnp.where(zk // 2 == y, 2, 0) + jnp.where(zk % 2 == core, 1, 0)
        other = lax.ppermute(shard, "row", over_x)
        piece = lax.dynamic_update_slice(piece, shard[None, None], (place, x, 0, 0))
        piece = lax.dynamic_update_slice(piece, other[None, None], (place, 1 - x, 0, 0))
        g_top = jnp.maximum(g_top, jnp.maximum(top(shard), top(other)))
        if k < 3:
            shard = lax.ppermute(shard, "row", next_z)
    piece = piece.reshape(4 * tokens, feats)

    bound = jnp.full((8, 128), jnp.maximum(feats * g_top * w_top, 1e-30))
    bound_sib = lax.ppermute(bound, "col", over_core)
    bound_pair = bound + bound_sib
    bound_far = lax.ppermute(bound_pair, "col", over_y)
    scale, from_sib = F16_TOP / bound[0, 0], bound_sib[0, 0] / F16_TOP
    to_far, from_far = F16_TOP / bound_pair[0, 0], bound_far[0, 0] / F16_TOP

    far_sib, far_mine = piece[:tokens], piece[tokens:2 * tokens]
    near_sib, near_mine = piece[2 * tokens:3 * tokens], piece[3 * tokens:]
    width = hidden // CHUNKS
    pairs = []
    for j in range(CHUNKS):
        w = w_down[j * width:(j + 1) * width]
        out = matmul_t(far_sib, w)
        back = lax.ppermute(out, "col", over_core)
        pair = matmul_t(far_mine, w) + back
        pairs.append((pair * to_far).astype(jnp.float16))
    arrived = [lax.ppermute(pair, "col", over_y) for pair in pairs[:-1]]

    act_far = gelu_value(pre_far.astype(jnp.float32)).astype(jnp.bfloat16)
    act_far, near_sib, _ = lax.optimization_barrier((act_far, near_sib, pairs[1]))
    act_far_sib = lax.ppermute(act_far, "col", over_core)

    near_out = (matmul_t(near_sib, w_down) * scale).astype(jnp.float16)
    near_back = lax.ppermute(near_out, "col", over_core)
    near = matmul_t(near_mine, w_down) + near_back.astype(jnp.float32) * from_sib

    act_full = jnp.concatenate([act_far_sib, act_far, act_near_sib, act_near], axis=0)
    grad_w = lax.dot_general(
        act_full, piece, (((0,), (0,)), ((), ())), preferred_element_type=jnp.float32
    )
    acc_new = acc_down + grad_w * float(total) ** (-0.5)

    last, acc_new = lax.optimization_barrier((pairs[-1], acc_new))
    arrived.append(lax.ppermute(last, "col", over_y))

    slope = gelu_slope(pre_act.astype(jnp.float32))
    parts = []
    for j in range(CHUNKS):
        cut = slice(j * width, (j + 1) * width)
        mine, factor, there = near[:, cut], slope[:, cut], arrived[j]
        if j == CHUNKS - 1:
            mine, factor, there, *parts = lax.optimization_barrier((mine, factor, there, *parts))
        both = mine + there.astype(jnp.float32) * from_far
        parts.append((both * factor).astype(jnp.bfloat16))
    return (acc_new, jnp.concatenate(parts, axis=1))


def solution(mesh):
    paired = mesh.shape["row"] == 8 and mesh.shape["col"] == 4
    return jax.shard_map(
        on_device_paired if paired else on_device_plain,
        mesh=mesh,
        in_specs=(P("row", "col"), P("row", "col"), P("col", "row"), P("row", "col")),
        out_specs=(P("row", "col"), P("col", "row")),
        check_vma=False,
    )
```
